32 devices in a mesh: groups: 2 (over y), traj: 16 (over z, x, core).
Axes of the slice: x: 2, y: 2, z: 4, core: 2. Of those that a mesh axis runs over, the one named last changes fastest.
Arguments:
- trajectories: bfloat16 [16384, 192], P(('groups', 'traj')), parts along dimension 0
- landmark_index: int32 [1024], P(('groups', 'traj')), parts along dimension 0, may hold values from 0 to 8191, as said below
- start_vectors: float32 [16384, 32], P(('groups', 'traj')), parts along dimension 0, may hold values from -6 to 6
Outputs:
- embedding: float32 [16384, 32], P(('groups', 'traj')), parts along dimension 0
The draws below stay inside these ranges and needn't reach their ends.
There are 2 independent parts, one for each index of `groups`. The reference program is written for one: setup_inputs(seed, part) draws one part's arguments, and reference() takes and returns one part's arrays. A program takes and returns all parts, laid end to end along the dimension named above; each array names one. Nothing has to cross between parts.
Inputs may be any that keep to these rules, and one draw needn't show every extreme that they name: `landmark_index`: entries b * 32 to (b + 1) * 32 - 1 are distinct rows of the range b * 512 to (b + 1) * 512 - 1, for every b.
All inputs are finite; a program needn't handle non-finite values.
Results may differ from the reference program's by a relative error of at most 0.0003.
Values may be sent and summed in bfloat16 or wider, within the bound.
A program may use at most 64 MiB of HBM per device.

```python
import math
import jax
import jax.numpy as jnp
from jax import lax

FEAT = 192
VECS = 32
SWEEPS = 2
ROW_DEV = 512
LM_DEV = 32
ROWS = 8192
LANDMARKS = 512


def draw_trajectories(key, part):
    keys = jax.random.split(key, 4)
    clusters = 64
    centers = jax.random.normal(keys[0], (clusters, FEAT), jnp.float32)
    labels = jax.random.randint(keys[1], (ROWS,), 0, clusters)
    spread = jnp.full((clusters,), 0.25, jnp.float32)
    noise = jax.random.normal(keys[3], (ROWS, FEAT), jnp.float32)
    values = centers[labels] + spread[labels][:, None] * noise
    return values.astype(jnp.bfloat16)


def draw_landmark_index(key, part):
    blocks = LANDMARKS // LM_DEV

    def one_block(block):
        order = jax.random.permutation(jax.random.fold_in(key, block), ROW_DEV)
        return block * ROW_DEV + order[:LM_DEV].astype(jnp.int32)
    picked = jax.vmap(one_block)(jnp.arange(blocks, dtype=jnp.int32))
    return picked.reshape(LANDMARKS).astype(jnp.int32)


def shard_levels(own_key, shape, cuts, low, high):
    gain, own = 1.0, jax.random.fold_in(own_key, 6)
    for axis_at, blocks in cuts:
        draws = jnp.exp(jax.random.uniform(jax.random.fold_in(own, axis_at), (blocks,), jnp.float32, low / len(cuts), high / len(cuts)))
        gain = gain * jnp.repeat(draws, shape[axis_at] // blocks).reshape([-1 if axis == axis_at else 1 for axis in range(len(shape))])
    return gain


def bell_draw(key, dims, scale, reach, cuts=(), held_as=jnp.bfloat16):
    entries = scale * jax.random.normal(key, dims, jnp.float32)
    if cuts:
        entries = entries * shard_levels(key, dims, cuts, -0.22, 0.18)
    return jnp.clip(entries, -reach, reach).astype(held_as)


def setup_inputs(seed: int = 0, part: int = 0) -> dict:
    streams_of = jax.random.split(jax.random.key(seed), 4)
    own_keys = jax.random.split(jax.random.fold_in(streams_of[3], part), 4)
    return {
        "trajectories": draw_trajectories(jax.random.fold_in(jax.random.fold_in(streams_of[3], part), 71), part),
        "landmark_index": draw_landmark_index(jax.random.fold_in(jax.random.fold_in(streams_of[3], part), 71), part),
        "start_vectors": bell_draw(own_keys[2], (ROWS, VECS), 1.0, 6.0, ((0, 16),), jnp.float32),
    }


HIGH = lax.Precision.HIGHEST

def kernel_block(rows, row_norms, lands, land_norms):
    cross = lax.dot_general(rows.astype(jnp.float32), lands.astype(jnp.float32), (((1,), (1,)), ((), ())), precision=HIGH, preferred_element_type=jnp.float32)
    dist = row_norms[:, None] + land_norms[None, :] - 2.0 * cross
    return jnp.exp(-dist * (2.0 / FEAT))

def land_blocks(lands, land_norms):
    width = math.gcd(lands.shape[0], 512)
    count = lands.shape[0] // width
    return (lands.reshape(count, width, lands.shape[1]), land_norms.reshape(count, width), count, width)

def column_pass(rows, row_norms, lands, land_norms, weighted):
    blocks, norms, count, width = land_blocks(lands, land_norms)

    def one_block(pair):
        block = kernel_block(rows, row_norms, pair[0], pair[1])
        return lax.dot_general(block.astype(jnp.float32), weighted.astype(jnp.float32), (((0,), (0,)), ((), ())), precision=HIGH, preferred_element_type=jnp.float32)
    parts = lax.map(one_block, (blocks, norms))
    return parts.reshape(lands.shape[0], weighted.shape[1])

def row_pass(rows, row_norms, lands, land_norms, mixing):
    blocks, norms, count, width = land_blocks(lands, land_norms)
    mixed = mixing.reshape(count, width, mixing.shape[1])

    def step_block(total, item):
        block = kernel_block(rows, row_norms, item[0], item[1])
        return (total + jnp.dot(block.astype(jnp.float32), item[2].astype(jnp.float32), precision=HIGH, preferred_element_type=jnp.float32), None)
    start = jnp.zeros((rows.shape[0], mixing.shape[1]), jnp.float32)
    total, unused = lax.scan(step_block, start, (blocks, norms, mixed))
    return total

def orthonormal(block, gram):
    lower = jnp.linalg.cholesky(gram)
    return jax.scipy.linalg.solve_triangular(lower, block.T, lower=True).T

def orthonormal_upper(block, gram):
    return orthonormal(block[:, ::-1], gram[::-1, ::-1])[:, ::-1]

def reference(trajectories, landmark_index, start_vectors):
    rows = trajectories.astype(jnp.float32)
    row_norms = lax.optimization_barrier(jnp.sum(rows * rows, axis=1))
    lands = jnp.take(rows, landmark_index, axis=0)
    land_norms = jnp.take(row_norms, landmark_index, axis=0)
    land_deg = row_pass(lands, land_norms, lands, land_norms, jnp.ones((LANDMARKS, 1), jnp.float32))
    col_sums = column_pass(rows, row_norms, lands, land_norms, jnp.ones((ROWS, 1), jnp.float32))
    degree = row_pass(rows, row_norms, lands, land_norms, col_sums / land_deg)
    dinv = lax.rsqrt(degree)
    vectors = start_vectors
    for sweep in range(SWEEPS):
        sums = column_pass(rows, row_norms, lands, land_norms, dinv * vectors)
        block = dinv * row_pass(rows, row_norms, lands, land_norms, sums / land_deg)
        gram = jnp.dot(block.T.astype(jnp.float32), block.astype(jnp.float32), precision=HIGH, preferred_element_type=jnp.float32)
        if sweep + 1 < SWEEPS:
            vectors = orthonormal_upper(block, gram)
        else:
            vectors = orthonormal(block, gram)
    return math.sqrt(ROWS) * vectors
```

```python
import functools
import math

import jax
import jax.numpy as jnp
from jax import lax
from jax.experimental import pallas as pl
from jax.experimental.pallas import tpu as pltpu
from jax.sharding import PartitionSpec as P

F32 = jnp.float32
BF16 = jnp.bfloat16
HIGH = lax.Precision.HIGHEST
MESH = pl.DeviceIdType.MESH
VECS = 32
OWN = 32
HALF = OWN // 2
NT = (((1,), (1,)), ((), ()))
NN = (((1,), (0,)), ((), ()))


def mxu(a, b, dims=NN):
    return lax.dot_general(a, b, dims, preferred_element_type=F32)


def exact(a, b, dims=NN):
    return lax.dot_general(a, b, dims, precision=HIGH, preferred_element_type=F32)


def split2(x):
    hi = x.astype(BF16)
    lo = (x - hi.astype(F32)).astype(BF16)
    return jnp.concatenate([hi, lo], axis=0)


def inverse_factor(gram, reverse):
    lane = lax.broadcasted_iota(jnp.int32, (8, 128), 1)
    sub = lax.broadcasted_iota(jnp.int32, (8, 128), 0)
    nblk = VECS // 8
    blocks = []
    for a in range(nblk):
        unit = (lane == sub + (VECS + 8 * a)).astype(F32)
        blocks.append(jnp.where(lane < VECS, gram[8 * a : 8 * a + 8, :], unit))
    order = range(VECS - 1, -1, -1) if reverse else range(VECS)
    for j in order:
        a, s = divmod(j, 8)
        pivot = blocks[a][s : s + 1, :]
        scaled = pivot * (1.0 / pivot[:, j : j + 1])
        for c in range(nblk):
            if (c > a and not reverse) or (c < a and reverse):
                blocks[c] = blocks[c] - blocks[c][:, j : j + 1] * scaled
            elif c == a:
                keep = sub < s if reverse else sub > s
                blocks[c] = blocks[c] - jnp.where(keep, blocks[c][:, j : j + 1], 0.0) * scaled
    done = []
    for a in range(nblk):
        diag = jnp.sum(jnp.where(lane == sub + 8 * a, blocks[a], 0.0), axis=1, keepdims=True)
        done.append(blocks[a] * lax.rsqrt(diag))
    whole = jnp.concatenate(done, axis=0)
    return whole[:, VECS : 2 * VECS]


def body(n, total_rows, xt_ref, idx_ref, qt_ref, out_ref,
         lsrc, lbuf, x_a, x_b, cmat, own_c, chi, clo, csrc, cbuf,
         z1, r1, t1, a1, z2, r2, t2, a2, gsrc, gbuf, send, recv):
    me = lax.axis_index("traj")
    rows = xt_ref.shape[1]
    feat = xt_ref.shape[0]
    rest = feat - 128
    lands = OWN * n
    side = HALF * n
    lt = lands // 128
    scale = 2.0 / feat

    def peer(d):
        return lax.rem(me + d, n)

    def spread(k, source, target):
        @pl.loop(1, n)
        def _(d):
            to = peer(d)
            pltpu.make_async_remote_copy(
                src_ref=source(to), dst_ref=target.at[me],
                send_sem=send.at[k], recv_sem=recv.at[k],
                device_id={"traj": to}, device_id_type=MESH,
            ).start()

    def arrived(k, target):
        part = target.at[pl.ds(0, n - 1)]
        pltpu.make_async_copy(part, part, recv.at[k]).wait()

    def left(k, target):
        part = target.at[pl.ds(0, n - 1)]
        pltpu.make_async_copy(part, part, send.at[k]).wait()

    barrier = pltpu.get_barrier_semaphore()

    @pl.loop(1, n)
    def _(d):
        pl.semaphore_signal(barrier, inc=1, device_id={"traj": peer(d)}, device_id_type=MESH)

    xt = xt_ref[...]
    gap = jnp.zeros((256 - feat, rows), BF16)
    xt_a = jnp.concatenate([xt, gap], axis=0)
    xt_b = jnp.concatenate([xt[:128], gap, xt[128:]], axis=0)
    idx = idx_ref[...] - me * rows
    eye = lax.broadcasted_iota(jnp.int32, (OWN, OWN), 0) == lax.broadcasted_iota(jnp.int32, (OWN, OWN), 1)
    idx_col = jnp.sum(jnp.where(eye, jnp.broadcast_to(idx, (OWN, OWN)).astype(F32), 0.0), axis=1, keepdims=True)
    spot = lax.broadcasted_iota(jnp.int32, (OWN, rows), 1).astype(F32)
    hot = (spot == idx_col).astype(F32).astype(BF16)
    own_a = mxu(hot, xt_a, NT)
    own_b = mxu(hot, xt_b, NT)
    lsrc[0] = own_a[:HALF, :128].astype(BF16)
    lsrc[1] = own_a[HALF:, :128].astype(BF16)
    lsrc[2] = (own_a[:HALF, 128:] + own_b[HALF:, 128:]).astype(BF16)

    pl.semaphore_wait(barrier, n - 1)
    spread(0, lambda to: lsrc, lbuf)
    lbuf[me] = lsrc[...]

    x_a[:rows] = jnp.transpose(xt_a)
    x_b[:rows] = jnp.transpose(xt_b)
    x_a[rows:] = own_a.astype(BF16)
    x_b[rows:] = own_b.astype(BF16)
    wide = x_a[...].astype(F32)
    row_norms = jnp.sum(wide * wide, axis=1, keepdims=True) * scale
    lane256 = lax.broadcasted_iota(jnp.int32, (16, 256), 1)
    mask_a = (lane256 < feat).astype(F32).astype(BF16)
    mask_b = ((lane256 < 128) | (lane256 >= 256 - rest)).astype(F32).astype(BF16)

    arrived(0, lbuf)
    width = min(side, 256)
    own_sum = jnp.zeros((OWN, 1), F32)
    for half, (x, mask) in enumerate(((x_a, mask_a), (x_b, mask_b))):
        for piece in range(side // width):
            blk = pl.ds(piece * (width // HALF), width // HALF)
            land = jnp.concatenate(
                [lbuf[blk, half].reshape(width, 128), lbuf[blk, 2].reshape(width, 128)], axis=1)
            lw = land.astype(F32)
            sq = lw * lw
            sq_hi = sq.astype(BF16)
            sq_lo = (sq - sq_hi.astype(F32)).astype(BF16)
            norm = (mxu(mask, sq_hi, NT) + mxu(mask, sq_lo, NT))[0:1] * scale
            cross = mxu(x[...], land, NT)
            block = jnp.exp(cross * (2.0 * scale) - (row_norms + norm))
            at = half * side + piece * width
            cmat[:, at : at + width] = block[:rows]
            sums = jnp.sum(block[:rows], axis=0, keepdims=True)
            for b in range(width // 128):
                csrc[at // 128 + b : at // 128 + b + 1, :] = sums[:, 128 * b : 128 * b + 128]
            own_sum = own_sum + jnp.sum(block[rows:], axis=1, keepdims=True)
    lane = lax.broadcasted_iota(jnp.int32, (OWN, 128), 1)
    sub = lax.broadcasted_iota(jnp.int32, (OWN, 128), 0)
    fit = (lane // HALF == lax.rem(me, 8)) & (lax.rem(lane, HALF) == lax.rem(sub, HALF))
    placed = jnp.where(fit, own_sum, 0.0)
    place_a = jnp.sum(placed[:HALF], axis=0, keepdims=True)
    place_b = jnp.sum(placed[HALF:], axis=0, keepdims=True)
    at_row = lax.broadcasted_iota(jnp.int32, (lt // 2, 128), 0) == me // 8
    csrc[lt : lt + lt // 2] = jnp.where(at_row, place_a, 0.0)
    csrc[lt + lt // 2 : 2 * lt] = jnp.where(at_row, place_b, 0.0)
    spread(1, lambda to: csrc, cbuf)
    cbuf[me] = csrc[...]

    for at in range(0, lands, 256):
        c = cmat[:, at : at + 256]
        hi = c.astype(BF16)
        chi[:, at : at + 256] = hi
        clo[:, at : at + 256] = (c - hi.astype(F32)).astype(BF16)

    def across_rows(left_rows):
        m = left_rows.shape[0]
        s = split2(left_rows)
        r = mxu(s, chi[...]) + mxu(s, clo[...])
        return r[:m] + r[m:]

    def across_lands(left_lands):
        m = left_lands.shape[0]
        s = split2(left_lands)
        r = mxu(s, chi[...], NT) + mxu(s, clo[...], NT)
        return r[:m] + r[m:]

    def as_row(x):
        return jnp.concatenate([x[b : b + 1, :] for b in range(lt)], axis=1)

    arrived(1, cbuf)
    sums = jnp.sum(cbuf[...], axis=0)
    inv = 1.0 / sums[lt:]
    inv_row = as_row(inv)
    ratio = as_row(sums[:lt] * inv)
    degree = across_lands(jnp.broadcast_to(ratio, (8, lands)))[0:1]
    dinv = lax.rsqrt(degree)

    def reduced(k, value, zs, rs, ts, gather):
        for a in range(VECS // 8):
            for b in range(lt):
                zs[a * lt + b] = value[8 * a : 8 * a + 8, 128 * b : 128 * b + 128]
        spread(k, lambda to: zs.at[to], rs)
        rs[me] = zs[me]
        arrived(k, rs)
        ts[...] = jnp.sum(rs[...], axis=0)
        spread(k + 1, lambda to: ts, gather)
        gather[me] = ts[...]
        arrived(k + 1, gather)
        return jnp.concatenate(
            [jnp.concatenate([gather[a * lt + b] for b in range(lt)], axis=1) for a in range(VECS // 8)], axis=0)

    sums1 = reduced(2, across_rows(qt_ref[...] * dinv), z1, r1, t1, a1)
    u1 = sums1 * inv_row
    y1 = across_lands(u1) * dinv
    sums2 = reduced(4, across_rows(y1 * dinv), z2, r2, t2, a2)
    gram1 = exact(u1, jnp.concatenate([sums2] * 4, axis=0), NT)
    back = inverse_factor(gram1, True)
    y2 = exact(back, across_lands(sums2 * inv_row) * dinv)
    gram2 = exact(y2, jnp.concatenate([y2] * 4, axis=0), NT)
    packed = jnp.zeros((8, 128), F32)
    lane8 = lax.broadcasted_iota(jnp.int32, (8, 128), 1)
    for a in range(VECS // 8):
        packed = packed + jnp.where(lane8 // VECS == a, gram2[8 * a : 8 * a + 8], 0.0)
    gsrc[...] = packed
    spread(6, lambda to: gsrc, gbuf)
    gbuf[me] = gsrc[...]
    arrived(6, gbuf)
    total = jnp.sum(gbuf[...], axis=0)
    gram2 = jnp.concatenate(
        [total if a == 0 else pltpu.roll(total, 128 - VECS * a, 1) for a in range(VECS // 8)], axis=0)
    last = inverse_factor(gram2, False) * math.sqrt(total_rows)
    out_ref[...] = exact(last, y2)
    for k, buf in enumerate((lbuf, cbuf, r1, a1, r2, a2, gbuf)):
        left(k, buf)


def local(trajectories, landmark_index, start_vectors):
    n = lax.axis_size("traj")
    rows, feat = trajectories.shape
    lands = OWN * n
    lt = lands // 128
    vmem = pl.BlockSpec(memory_space=pltpu.VMEM)
    tiles = pltpu.VMEM((n, 8, 128), F32)
    tile = pltpu.VMEM((8, 128), F32)
    out = pl.pallas_call(
        functools.partial(body, n, rows * n),
        out_shape=jax.ShapeDtypeStruct((VECS, rows), F32),
        in_specs=[vmem] * 3,
        out_specs=vmem,
        scratch_shapes=[
            pltpu.VMEM((3, HALF, 128), BF16),
            pltpu.VMEM((n, 3, HALF, 128), BF16),
            pltpu.VMEM((rows + OWN, 256), BF16),
            pltpu.VMEM((rows + OWN, 256), BF16),
            pltpu.VMEM((rows, lands), F32),
            tile,
            pltpu.VMEM((rows, lands), BF16),
            pltpu.VMEM((rows, lands), BF16),
            pltpu.VMEM((2 * lt, 128), F32),
            pltpu.VMEM((n, 2 * lt, 128), F32),
            tiles, tiles, tile, tiles,
            tiles, tiles, tile, tiles,
            tile, tiles,
            pltpu.SemaphoreType.DMA((7,)),
            pltpu.SemaphoreType.DMA((7,)),
        ],
        compiler_params=pltpu.CompilerParams(
            collective_id=0, has_side_effects=True, vmem_limit_bytes=48 * 1024 * 1024),
        cost_estimate=pl.CostEstimate(flops=10**9, bytes_accessed=10**6, transcendentals=10**6),
    )(trajectories.T, landmark_index.reshape(1, OWN), start_vectors.T)
    return out.T


def solution(mesh):
    return jax.shard_map(
        local,
        mesh=mesh,
        in_specs=(P(("groups", "traj"), None), P(("groups", "traj")), P(("groups", "traj"), None)),
        out_specs=P(("groups", "traj"), None),
        check_vma=False,
    )
```

```python
import functools
import math

import jax
import jax.numpy as jnp
from jax import lax
from jax.experimental import pallas as pl
from jax.experimental.pallas import tpu as pltpu
from jax.sharding import PartitionSpec as P

F32 = jnp.float32
BF16 = jnp.bfloat16
HIGH = lax.Precision.HIGHEST
MESH = pl.DeviceIdType.MESH
VECS = 32
OWN = 32
HALF = OWN // 2
NT = (((1,), (1,)), ((), ()))
NN = (((1,), (0,)), ((), ()))


def mxu(a, b, dims=NN):
    return lax.dot_general(a, b, dims, preferred_element_type=F32)


def exact(a, b, dims=NN):
    return lax.dot_general(a, b, dims, precision=HIGH, preferred_element_type=F32)


def split2(x):
    hi = x.astype(BF16)
    lo = (x - hi.astype(F32)).astype(BF16)
    return jnp.concatenate([hi, lo], axis=0)


def inverse_factor(gram, reverse):
    lane = lax.broadcasted_iota(jnp.int32, (8, 128), 1)
    sub = lax.broadcasted_iota(jnp.int32, (8, 128), 0)
    nblk = VECS // 8
    blocks = []
    for a in range(nblk):
        unit = (lane == sub + (VECS + 8 * a)).astype(F32)
        blocks.append(jnp.where(lane < VECS, gram[8 * a : 8 * a + 8, :], unit))
    for a in range(nblk - 1, -1, -1) if reverse else range(nblk):
        others = range(a + 1) if reverse else range(a, nblk)
        columns = {
            (c, u): jnp.broadcast_to(blocks[c][:, 8 * a + u : 8 * a + u + 1], (8, 128)) for u in range(8) for c in others
        }
        for t in range(7, -1, -1) if reverse else range(8):
            inner = range(t) if reverse else range(t + 1, 8)
            keep = sub < t if reverse else sub > t
            turn = 1.0 / columns[a, t][t : t + 1, :]
            pivot = blocks[a][t : t + 1, :]
            tops = {u: columns[a, u][t : t + 1, :] for u in inner}
            for c in others:
                factor = columns[c, t] * turn
                if c == a:
                    factor = jnp.where(keep, factor, 0.0)
                for u in inner:
                    columns[c, u] = columns[c, u] - factor * tops[u]
                blocks[c] = blocks[c] - factor * pivot
    done = []
    for a in range(nblk):
        diag = jnp.sum(jnp.where(lane == sub + 8 * a, blocks[a], 0.0), axis=1, keepdims=True)
        done.append(blocks[a] * lax.rsqrt(diag))
    whole = jnp.concatenate(done, axis=0)
    return whole[:, VECS : 2 * VECS]


def body(n, total_rows, xt_ref, idx_ref, qt_ref, out_ref,
         lsrc, lbuf, x_a, x_b, cmat, own_c, chi, clo, csrc, cbuf,
         z1, r1, t1, a1, z2, r2, t2, a2, gsrc, gbuf, send, recv):
    me = lax.axis_index("traj")
    rows = xt_ref.shape[1]
    feat = xt_ref.shape[0]
    rest = feat - 128
    lands = OWN * n
    side = HALF * n
    lt = lands // 128
    scale = 2.0 / feat

    def peer(d):
        return lax.rem(me + d, n)

    def spread(k, source, target):
        @pl.loop(1, n)
        def _(d):
            to = peer(d)
            pltpu.make_async_remote_copy(
                src_ref=source(to), dst_ref=target.at[me],
                send_sem=send.at[k], recv_sem=recv.at[k],
                device_id={"traj": to}, device_id_type=MESH,
            ).start()

    def arrived(k, target):
        part = target.at[pl.ds(0, n - 1)]
        pltpu.make_async_copy(part, part, recv.at[k]).wait()

    def left(k, target):
        part = target.at[pl.ds(0, n - 1)]
        pltpu.make_async_copy(part, part, send.at[k]).wait()

    barrier = pltpu.get_barrier_semaphore()

    @pl.loop(1, n)
    def _(d):
        pl.semaphore_signal(barrier, inc=1, device_id={"traj": peer(d)}, device_id_type=MESH)

    xt = xt_ref[...]
    gap = jnp.zeros((256 - feat, rows), BF16)
    xt_a = jnp.concatenate([xt, gap], axis=0)
    xt_b = jnp.concatenate([xt[:128], gap, xt[128:]], axis=0)
    idx = idx_ref[...] - me * rows
    eye = lax.broadcasted_iota(jnp.int32, (OWN, OWN), 0) == lax.broadcasted_iota(jnp.int32, (OWN, OWN), 1)
    idx_col = jnp.sum(jnp.where(eye, jnp.broadcast_to(idx, (OWN, OWN)).astype(F32), 0.0), axis=1, keepdims=True)
    spot = lax.broadcasted_iota(jnp.int32, (OWN, rows), 1).astype(F32)
    hot = (spot == idx_col).astype(F32).astype(BF16)
    own_a = mxu(hot, xt_a, NT)
    own_b = mxu(hot, xt_b, NT)
    lsrc[0] = own_a[:HALF, :128].astype(BF16)
    lsrc[1] = own_a[HALF:, :128].astype(BF16)
    lsrc[2] = (own_a[:HALF, 128:] + own_b[HALF:, 128:]).astype(BF16)

    pl.semaphore_wait(barrier, n - 1)
    spread(0, lambda to: lsrc, lbuf)
    lbuf[me] = lsrc[...]

    x_a[:rows] = jnp.transpose(xt_a)
    x_b[:rows] = jnp.transpose(xt_b)
    x_a[rows:] = own_a.astype(BF16)
    x_b[rows:] = own_b.astype(BF16)
    wide = x_a[...].astype(F32)
    row_norms = jnp.sum(wide * wide, axis=1, keepdims=True) * scale
    lane256 = lax.broadcasted_iota(jnp.int32, (16, 256), 1)
    mask_a = (lane256 < feat).astype(F32).astype(BF16)
    mask_b = ((lane256 < 128) | (lane256 >= 256 - rest)).astype(F32).astype(BF16)

    arrived(0, lbuf)
    width = min(side, 256)
    own_sum = jnp.zeros((OWN, 1), F32)
    for half, (x, mask) in enumerate(((x_a, mask_a), (x_b, mask_b))):
        for piece in range(side // width):
            blk = pl.ds(piece * (width // HALF), width // HALF)
            land = jnp.concatenate(
                [lbuf[blk, half].reshape(width, 128), lbuf[blk, 2].reshape(width, 128)], axis=1)
            lw = land.astype(F32)
            sq = lw * lw
            sq_hi = sq.astype(BF16)
            sq_lo = (sq - sq_hi.astype(F32)).astype(BF16)
            norm = (mxu(mask, sq_hi, NT) + mxu(mask, sq_lo, NT))[0:1] * scale
            cross = mxu(x[...], land, NT)
            block = jnp.exp(cross * (2.0 * scale) - (row_norms + norm))
            at = half * side + piece * width
            cmat[:, at : at + width] = block[:rows]
            sums = jnp.sum(block[:rows], axis=0, keepdims=True)
            for b in range(width // 128):
                csrc[at // 128 + b : at // 128 + b + 1, :] = sums[:, 128 * b : 128 * b + 128]
            own_sum = own_sum + jnp.sum(block[rows:], axis=1, keepdims=True)
    lane = lax.broadcasted_iota(jnp.int32, (OWN, 128), 1)
    sub = lax.broadcasted_iota(jnp.int32, (OWN, 128), 0)
    fit = (lane // HALF == lax.rem(me, 8)) & (lax.rem(lane, HALF) == lax.rem(sub, HALF))
    placed = jnp.where(fit, own_sum, 0.0)
    place_a = jnp.sum(placed[:HALF], axis=0, keepdims=True)
    place_b = jnp.sum(placed[HALF:], axis=0, keepdims=True)
    at_row = lax.broadcasted_iota(jnp.int32, (lt // 2, 128), 0) == me // 8
    csrc[lt : lt + lt // 2] = jnp.where(at_row, place_a, 0.0)
    csrc[lt + lt // 2 : 2 * lt] = jnp.where(at_row, place_b, 0.0)
    spread(1, lambda to: csrc, cbuf)
    cbuf[me] = csrc[...]

    for at in range(0, lands, 256):
        c = cmat[:, at : at + 256]
        hi = c.astype(BF16)
        chi[:, at : at + 256] = hi
        clo[:, at : at + 256] = (c - hi.astype(F32)).astype(BF16)

    def across_rows(left_rows):
        m = left_rows.shape[0]
        s = split2(left_rows)
        r = mxu(s, chi[...]) + mxu(s, clo[...])
        return r[:m] + r[m:]

    def across_lands(left_lands):
        m = left_lands.shape[0]
        s = split2(left_lands)
        r = mxu(s, chi[...], NT) + mxu(s, clo[...], NT)
        return r[:m] + r[m:]

    def as_row(x):
        return jnp.concatenate([x[b : b + 1, :] for b in range(lt)], axis=1)

    arrived(1, cbuf)
    sums = jnp.sum(cbuf[...], axis=0)
    inv = 1.0 / sums[lt:]
    inv_row = as_row(inv)
    ratio = as_row(sums[:lt] * inv)
    degree = across_lands(jnp.broadcast_to(ratio, (8, lands)))[0:1]
    dinv = lax.rsqrt(degree)

    def reduced(k, value, zs, rs, ts, gather):
        for a in range(VECS // 8):
            for b in range(lt):
                zs[a * lt + b] = value[8 * a : 8 * a + 8, 128 * b : 128 * b + 128]
        spread(k, lambda to: zs.at[to], rs)
        rs[me] = zs[me]
        arrived(k, rs)
        ts[...] = jnp.sum(rs[...], axis=0)
        spread(k + 1, lambda to: ts, gather)
        gather[me] = ts[...]
        arrived(k + 1, gather)
        return jnp.concatenate(
            [jnp.concatenate([gather[a * lt + b] for b in range(lt)], axis=1) for a in range(VECS // 8)], axis=0)

    sums1 = reduced(2, across_rows(qt_ref[...] * dinv), z1, r1, t1, a1)
    u1 = sums1 * inv_row
    y1 = across_lands(u1) * dinv
    sums2 = reduced(4, across_rows(y1 * dinv), z2, r2, t2, a2)
    y2 = across_lands(sums2 * inv_row) * dinv
    gram2 = exact(y2, jnp.concatenate([y2] * 4, axis=0), NT)
    packed = jnp.zeros((8, 128), F32)
    lane8 = lax.broadcasted_iota(jnp.int32, (8, 128), 1)
    for a in range(VECS // 8):
        packed = packed + jnp.where(lane8 // VECS == a, gram2[8 * a : 8 * a + 8], 0.0)
    gsrc[...] = packed
    spread(6, lambda to: gsrc, gbuf)
    gbuf[me] = gsrc[...]
    back = inverse_factor(exact(u1, jnp.concatenate([sums2] * 4, axis=0), NT), True)
    arrived(6, gbuf)
    total = jnp.sum(gbuf[...], axis=0)
    gram2 = jnp.concatenate(
        [total if a == 0 else pltpu.roll(total, 128 - VECS * a, 1) for a in range(VECS // 8)], axis=0)[:, :VECS]
    gram2 = exact(exact(back, gram2), jnp.concatenate([back] * 4, axis=0), NT)
    last = exact(inverse_factor(gram2, False) * math.sqrt(total_rows), back)
    out_ref[...] = exact(last, y2)
    for k, buf in enumerate((lbuf, cbuf, r1, a1, r2, a2, gbuf)):
        left(k, buf)


def local(trajectories, landmark_index, start_vectors):
    n = lax.axis_size("traj")
    rows, feat = trajectories.shape
    lands = OWN * n
    lt = lands // 128
    vmem = pl.BlockSpec(memory_space=pltpu.VMEM)
    tiles = pltpu.VMEM((n, 8, 128), F32)
    tile = pltpu.VMEM((8, 128), F32)
    out = pl.pallas_call(
        functools.partial(body, n, rows * n),
        out_shape=jax.ShapeDtypeStruct((VECS, rows), F32),
        in_specs=[vmem] * 3,
        out_specs=vmem,
        scratch_shapes=[
            pltpu.VMEM((3, HALF, 128), BF16),
            pltpu.VMEM((n, 3, HALF, 128), BF16),
            pltpu.VMEM((rows + OWN, 256), BF16),
            pltpu.VMEM((rows + OWN, 256), BF16),
            pltpu.VMEM((rows, lands), F32),
            tile,
            pltpu.VMEM((rows, lands), BF16),
            pltpu.VMEM((rows, lands), BF16),
            pltpu.VMEM((2 * lt, 128), F32),
            pltpu.VMEM((n, 2 * lt, 128), F32),
            tiles, tiles, tile, tiles,
            tiles, tiles, tile, tiles,
            tile, tiles,
            pltpu.SemaphoreType.DMA((7,)),
            pltpu.SemaphoreType.DMA((7,)),
        ],
        compiler_params=pltpu.CompilerParams(
            collective_id=0, has_side_effects=True, vmem_limit_bytes=48 * 1024 * 1024),
        cost_estimate=pl.CostEstimate(flops=10**9, bytes_accessed=10**6, transcendentals=10**6),
    )(trajectories.T, landmark_index.reshape(1, OWN), start_vectors.T)
    return out.T


def solution(mesh):
    return jax.shard_map(
        local,
        mesh=mesh,
        in_specs=(P(("groups", "traj"), None), P(("groups", "traj")), P(("groups", "traj"), None)),
        out_specs=P(("groups", "traj"), None),
        check_vma=False,
    )
```

```python
import functools
import math

import jax
import jax.numpy as jnp
from jax import lax
from jax.experimental import pallas as pl
from jax.experimental.pallas import tpu as pltpu
from jax.sharding import PartitionSpec as P

F32 = jnp.float32
BF16 = jnp.bfloat16
HIGH = lax.Precision.HIGHEST
MESH = pl.DeviceIdType.MESH
VECS = 32
OWN = 32
HALF = OWN // 2
NT = (((1,), (1,)), ((), ()))
NN = (((1,), (0,)), ((), ()))


def mxu(a, b, dims=NN):
    return lax.dot_general(a, b, dims, preferred_element_type=F32)


def exact(a, b, dims=NN):
    return lax.dot_general(a, b, dims, precision=HIGH, preferred_element_type=F32)


def split2(x):
    hi = x.astype(BF16)
    lo = (x - hi.astype(F32)).astype(BF16)
    return jnp.concatenate([hi, lo], axis=0)


def inverse_factor(gram, reverse):
    lane = lax.broadcasted_iota(jnp.int32, (8, 128), 1)
    sub = lax.broadcasted_iota(jnp.int32, (8, 128), 0)
    nblk = VECS // 8
    blocks = []
    for a in range(nblk):
        unit = (lane == sub + (VECS + 8 * a)).astype(F32)
        blocks.append(jnp.where(lane < VECS, gram[8 * a : 8 * a + 8, :], unit))
    for a in range(nblk - 1, -1, -1) if reverse else range(nblk):
        others = range(a + 1) if reverse else range(a, nblk)
        columns = {
            (c, u): jnp.broadcast_to(blocks[c][:, 8 * a + u : 8 * a + u + 1], (8, 128)) for u in range(8) for c in others
        }
        for t in range(7, -1, -1) if reverse else range(8):
            inner = range(t) if reverse else range(t + 1, 8)
            keep = sub < t if reverse else sub > t
            turn = 1.0 / columns[a, t][t : t + 1, :]
            pivot = blocks[a][t : t + 1, :]
            tops = {u: columns[a, u][t : t + 1, :] for u in inner}
            for c in others:
                factor = columns[c, t] * turn
                if c == a:
                    factor = jnp.where(keep, factor, 0.0)
                for u in inner:
                    columns[c, u] = columns[c, u] - factor * tops[u]
                blocks[c] = blocks[c] - factor * pivot
    done = []
    for a in range(nblk):
        diag = jnp.sum(jnp.where(lane == sub + 8 * a, blocks[a], 0.0), axis=1, keepdims=True)
        done.append(blocks[a] * lax.rsqrt(diag))
    whole = jnp.concatenate(done, axis=0)
    return whole[:, VECS : 2 * VECS]


def body(n, total_rows, xt_ref, idx_ref, qt_ref, out_ref,
         lsrc, lbuf, x_a, x_b, cmat, own_c, chi, clo, csrc, cbuf,
         z1, r1, t1, a1, z2, r2, t2, a2, gsrc, gbuf, send, recv):
    me = lax.axis_index("traj")
    rows = xt_ref.shape[1]
    feat = xt_ref.shape[0]
    rest = feat - 128
    lands = OWN * n
    side = HALF * n
    lt = lands // 128
    scale = 2.0 / feat

    def peer(d):
        return lax.rem(me + d, n)

    def spread(k, source, target):
        @pl.loop(1, n)
        def _(d):
            to = peer(d)
            pltpu.make_async_remote_copy(
                src_ref=source(to), dst_ref=target.at[me],
                send_sem=send.at[k], recv_sem=recv.at[k],
                device_id={"traj": to}, device_id_type=MESH,
            ).start()

    def arrived(k, target):
        part = target.at[pl.ds(0, n - 1)]
        pltpu.make_async_copy(part, part, recv.at[k]).wait()

    def left(k, target):
        part = target.at[pl.ds(0, n - 1)]
        pltpu.make_async_copy(part, part, send.at[k]).wait()

    barrier = pltpu.get_barrier_semaphore()

    @pl.loop(1, n)
    def _(d):
        pl.semaphore_signal(barrier, inc=1, device_id={"traj": peer(d)}, device_id_type=MESH)

    xt = xt_ref[...]
    gap = jnp.zeros((256 - feat, rows), BF16)
    xt_a = jnp.concatenate([xt, gap], axis=0)
    xt_b = jnp.concatenate([xt[:128], gap, xt[128:]], axis=0)
    idx = idx_ref[...] - me * rows
    eye = lax.broadcasted_iota(jnp.int32, (OWN, OWN), 0) == lax.broadcasted_iota(jnp.int32, (OWN, OWN), 1)
    idx_col = jnp.sum(jnp.where(eye, jnp.broadcast_to(idx, (OWN, OWN)).astype(F32), 0.0), axis=1, keepdims=True)
    spot = lax.broadcasted_iota(jnp.int32, (OWN, rows), 1).astype(F32)
    hot = (spot == idx_col).astype(F32).astype(BF16)
    own_a = mxu(hot, xt_a, NT)
    own_b = mxu(hot, xt_b, NT)
    lsrc[0] = own_a[:HALF, :128].astype(BF16)
    lsrc[1] = own_a[HALF:, :128].astype(BF16)
    lsrc[2] = (own_a[:HALF, 128:] + own_b[HALF:, 128:]).astype(BF16)

    pl.semaphore_wait(barrier, n - 1)
    spread(0, lambda to: lsrc, lbuf)
    lbuf[me] = lsrc[...]

    x_a[:rows] = jnp.transpose(xt_a)
    x_b[:rows] = jnp.transpose(xt_b)
    x_a[rows:] = own_a.astype(BF16)
    x_b[rows:] = own_b.astype(BF16)
    wide = x_a[...].astype(F32)
    row_norms = jnp.sum(wide * wide, axis=1, keepdims=True) * scale
    lane256 = lax.broadcasted_iota(jnp.int32, (16, 256), 1)
    mask_a = (lane256 < feat).astype(F32).astype(BF16)
    mask_b = ((lane256 < 128) | (lane256 >= 256 - rest)).astype(F32).astype(BF16)

    arrived(0, lbuf)
    width = min(side, 256)
    own_sum = jnp.zeros((OWN, 1), F32)
    for half, (x, mask) in enumerate(((x_a, mask_a), (x_b, mask_b))):
        for piece in range(side // width):
            blk = pl.ds(piece * (width // HALF), width // HALF)
            land = jnp.concatenate(
                [lbuf[blk, half].reshape(width, 128), lbuf[blk, 2].reshape(width, 128)], axis=1)
            lw = land.astype(F32)
            sq = lw * lw
            sq_hi = sq.astype(BF16)
            sq_lo = (sq - sq_hi.astype(F32)).astype(BF16)
            norm = (mxu(mask, sq_hi, NT) + mxu(mask, sq_lo, NT))[0:1] * scale
            cross = mxu(x[...], land, NT)
            block = jnp.exp(cross * (2.0 * scale) - (row_norms + norm))
            at = half * side + piece * width
            cmat[:, at : at + width] = block[:rows]
            sums = jnp.sum(block[:rows], axis=0, keepdims=True)
            for b in range(width // 128):
                csrc[at // 128 + b : at // 128 + b + 1, :] = sums[:, 128 * b : 128 * b + 128]
            own_sum = own_sum + jnp.sum(block[rows:], axis=1, keepdims=True)
    lane = lax.broadcasted_iota(jnp.int32, (OWN, 128), 1)
    sub = lax.broadcasted_iota(jnp.int32, (OWN, 128), 0)
    fit = (lane // HALF == lax.rem(me, 8)) & (lax.rem(lane, HALF) == lax.rem(sub, HALF))
    placed = jnp.where(fit, own_sum, 0.0)
    place_a = jnp.sum(placed[:HALF], axis=0, keepdims=True)
    place_b = jnp.sum(placed[HALF:], axis=0, keepdims=True)
    at_row = lax.broadcasted_iota(jnp.int32, (lt // 2, 128), 0) == me // 8
    csrc[lt : lt + lt // 2] = jnp.where(at_row, place_a, 0.0)
    csrc[lt + lt // 2 : 2 * lt] = jnp.where(at_row, place_b, 0.0)
    spread(1, lambda to: csrc, cbuf)
    cbuf[me] = csrc[...]

    for at in range(0, lands, 256):
        c = cmat[:, at : at + 256]
        hi = c.astype(BF16)
        chi[:, at : at + 256] = hi
        clo[:, at : at + 256] = (c - hi.astype(F32)).astype(BF16)

    def across_rows(left_rows):
        m = left_rows.shape[0]
        s = split2(left_rows)
        r = mxu(s, chi[...]) + mxu(s, clo[...])
        return r[:m] + r[m:]

    def across_lands(left_lands):
        m = left_lands.shape[0]
        s = split2(left_lands)
        r = mxu(s, chi[...], NT) + mxu(s, clo[...], NT)
        return r[:m] + r[m:]

    def as_row(x):
        return jnp.concatenate([x[b : b + 1, :] for b in range(lt)], axis=1)

    arrived(1, cbuf)
    sums = jnp.sum(cbuf[...], axis=0)
    inv = 1.0 / sums[lt:]
    inv_row = as_row(inv)
    ratio = as_row(sums[:lt] * inv)
    degree = across_lands(jnp.broadcast_to(ratio, (8, lands)))[0:1]
    dinv = lax.rsqrt(degree)

    def reduced(k, value, zs, rs, ts, gather):
        for a in range(VECS // 8):
            for b in range(lt):
                zs[a * lt + b] = value[8 * a : 8 * a + 8, 128 * b : 128 * b + 128]
        spread(k, lambda to: zs.at[to], rs)
        rs[me] = zs[me]
        arrived(k, rs)
        ts[...] = jnp.sum(rs[...], axis=0)
        spread(k + 1, lambda to: ts, gather)
        gather[me] = ts[...]
        arrived(k + 1, gather)
        return jnp.concatenate(
            [jnp.concatenate([gather[a * lt + b] for b in range(lt)], axis=1) for a in range(VECS // 8)], axis=0)

    sums1 = reduced(2, across_rows(qt_ref[...] * dinv), z1, r1, t1, a1)
    u1 = sums1 * inv_row
    y1 = across_lands(u1) * dinv
    sums2 = reduced(4, across_rows(y1 * dinv), z2, r2, t2, a2)
    y2 = across_lands(sums2 * inv_row) * dinv
    gram2 = exact(y2, jnp.concatenate([y2] * 4, axis=0), NT)
    packed = jnp.zeros((8, 128), F32)
    lane8 = lax.broadcasted_iota(jnp.int32, (8, 128), 1)
    for a in range(VECS // 8):
        packed = packed + jnp.where(lane8 // VECS == a, gram2[8 * a : 8 * a + 8], 0.0)
    gsrc[...] = packed
    spread(6, lambda to: gsrc, gbuf)
    gbuf[me] = gsrc[...]
    back = inverse_factor(exact(u1, jnp.concatenate([sums2] * 4, axis=0), NT), True)
    y2 = exact(back, y2) * math.sqrt(total_rows)
    arrived(6, gbuf)
    total = jnp.sum(gbuf[...], axis=0)
    gram2 = jnp.concatenate(
        [total if a == 0 else pltpu.roll(total, 128 - VECS * a, 1) for a in range(VECS // 8)], axis=0)[:, :VECS]
    gram2 = exact(exact(back, gram2), jnp.concatenate([back] * 4, axis=0), NT)
    out_ref[...] = exact(inverse_factor(gram2, False), y2)
    for k, buf in enumerate((lbuf, cbuf, r1, a1, r2, a2, gbuf)):
        left(k, buf)


def local(trajectories, landmark_index, start_vectors):
    n = lax.axis_size("traj")
    rows, feat = trajectories.shape
    lands = OWN * n
    lt = lands // 128
    vmem = pl.BlockSpec(memory_space=pltpu.VMEM)
    tiles = pltpu.VMEM((n, 8, 128), F32)
    tile = pltpu.VMEM((8, 128), F32)
    out = pl.pallas_call(
        functools.partial(body, n, rows * n),
        out_shape=jax.ShapeDtypeStruct((VECS, rows), F32),
        in_specs=[vmem] * 3,
        out_specs=vmem,
        scratch_shapes=[
            pltpu.VMEM((3, HALF, 128), BF16),
            pltpu.VMEM((n, 3, HALF, 128), BF16),
            pltpu.VMEM((rows + OWN, 256), BF16),
            pltpu.VMEM((rows + OWN, 256), BF16),
            pltpu.VMEM((rows, lands), F32),
            tile,
            pltpu.VMEM((rows, lands), BF16),
            pltpu.VMEM((rows, lands), BF16),
            pltpu.VMEM((2 * lt, 128), F32),
            pltpu.VMEM((n, 2 * lt, 128), F32),
            tiles, tiles, tile, tiles,
            tiles, tiles, tile, tiles,
            tile, tiles,
            pltpu.SemaphoreType.DMA((7,)),
            pltpu.SemaphoreType.DMA((7,)),
        ],
        compiler_params=pltpu.CompilerParams(
            collective_id=0, has_side_effects=True, vmem_limit_bytes=48 * 1024 * 1024),
        cost_estimate=pl.CostEstimate(flops=10**9, bytes_accessed=10**6, transcendentals=10**6),
    )(trajectories.T, landmark_index.reshape(1, OWN), start_vectors.T)
    return out.T


def solution(mesh):
    return jax.shard_map(
        local,
        mesh=mesh,
        in_specs=(P(("groups", "traj"), None), P(("groups", "traj")), P(("groups", "traj"), None)),
        out_specs=P(("groups", "traj"), None),
        check_vma=False,
    )
```
